32 devices in a mesh: req: 4 (over y, core), hid: 8 (over z, x).
Axes of the slice: x: 2, y: 2, z: 4, core: 2. Of those that a mesh axis runs over, the one named last changes fastest.
Arguments:
- tokens: bfloat16 [6144, 1536], P(('req', 'hid')), may hold values from -6 to 6
- segment: int32 [6144], P(('req', 'hid')), may hold values from 0 to 15, as said below
- attn_gain: float32 [1536], replicated, may hold values from 0.1 to 1.9
- w_query: bfloat16 [1536, 1536], replicated, may hold values from -0.2 to 0.2
- w_key: bfloat16 [1536, 512], replicated, may hold values from -0.2 to 0.2
- w_value: bfloat16 [1536, 512], replicated, may hold values from -0.15625 to 0.15625
- q_gain: float32 [64], replicated, may hold values from 0.5 to 6
- k_gain: float32 [64], replicated, may hold values from 0.5 to 6
- w_out: bfloat16 [1536, 1536], replicated, may hold values from -0.15625 to 0.15625
- ffn_gain: float32 [1536], replicated, may hold values from 0.1 to 1.9
- w_gate: bfloat16 [4608, 1536], P(('req', 'hid')), may hold values from -0.15625 to 0.15625
- w_up: bfloat16 [4608, 1536], P(('req', 'hid')), may hold values from -0.15625 to 0.15625
- w_down: bfloat16 [4608, 1536], P(('req', 'hid')), may hold values from -0.09375 to 0.09375
Outputs:
- mixed: bfloat16 [6144, 1536], P(('req', 'hid'))
- kv_cache: bfloat16 [6144, 1024], P(('req', 'hid'))
The draws below stay inside these ranges and needn't reach their ends.
Inputs may be any that keep to these rules, and one draw needn't show every extreme that they name: Segment ids never fall along the tokens and start at 0. A segment never crosses a boundary between aligned blocks of 1536 tokens; the first block is one segment of exactly 1536 tokens, and every later block holds exactly five segments.
All inputs are finite; a program needn't handle non-finite values.
Results may differ from the reference program's by a relative error of at most 0.015.
Values may be sent and summed in bfloat16 or wider, within the bound.
A program may use at most 128 MiB of HBM per device.

```python
import jax
import jax.numpy as jnp
from jax import lax

D = 1536
H = 24
KVH = 8
HD = 64
FF = 4608
GROUP_TOK = 1536
TOKENS = 6144
N_REQ = 4


def block_starts(block_key, block_pos):
    picks = jax.random.permutation(block_key, GROUP_TOK - 1)[:4].astype(jnp.int32) + 1
    hits = jnp.any(block_pos[:, None] == picks[None, :], axis=1)
    return hits | (block_pos == 0)


def draw_segment(key, part):
    block_count = TOKENS // GROUP_TOK
    block_pos = jnp.arange(GROUP_TOK, dtype=jnp.int32)
    block_keys = jax.random.split(jax.random.fold_in(key, 5), block_count)
    flags = jax.vmap(lambda k: block_starts(k, block_pos))(block_keys)
    first_row = (block_pos == 0)[None, :]
    block_idx = jnp.arange(block_count, dtype=jnp.int32)[:, None]
    flags = jnp.where(block_idx == 0, first_row, flags).reshape(TOKENS)
    return (jnp.cumsum(flags.astype(jnp.int32)) - 1).astype(jnp.int32)


def draw_tokens(key, part):
    noise_key = jax.random.fold_in(jax.random.fold_in(key, 11), 0)
    base = jax.random.normal(noise_key, (TOKENS, D), jnp.float32)
    return jnp.clip(base, -6.0, 6.0).astype(jnp.bfloat16)


def draw_w_query(key, part):
    own = jax.random.normal(jax.random.fold_in(key, 1), (D, H * HD), jnp.float32) * D ** (-0.5)
    return jnp.clip(own, -0.199, 0.199).astype(jnp.bfloat16)


def draw_w_key(key, part):
    own = jax.random.normal(jax.random.fold_in(key, 2), (D, KVH * HD), jnp.float32) * D ** (-0.5)
    return jnp.clip(own, -0.199, 0.199).astype(jnp.bfloat16)


def draw_q_gain(key, part):
    return jnp.exp(jax.random.uniform(jax.random.fold_in(key, 21), (HD,), jnp.float32, -0.693, 0.693))


def draw_k_gain(key, part):
    return jnp.exp(jax.random.uniform(jax.random.fold_in(key, 22), (HD,), jnp.float32, -0.693, 0.693))


def block_scale(own_key, shape, cuts, low, largest):
    level, own = 1.0, jax.random.fold_in(own_key, 6)
    for dim, shards_of in cuts:
        draws = jnp.exp(jax.random.uniform(jax.random.fold_in(own, dim), (shards_of,), jnp.float32, low / len(cuts), largest / len(cuts)))
        level = level * jnp.repeat(draws, shape[dim] // shards_of).reshape([-1 if axis == dim else 1 for axis in range(len(shape))])
    return level


def bell_draw(key, extent, scale, reach, shards=(), held_as=jnp.bfloat16):
    result = jax.random.normal(key, extent, jnp.float32) * scale
    if len(shards) > 0:
        result = block_scale(key, extent, shards, -0.22, 0.18) * result
    return jnp.clip(result, min=-reach, max=reach).astype(held_as)


def setup_inputs(seed: int = 0) -> dict:
    streams_of = jax.random.split(jax.random.key(seed), 14)
    tokens = draw_tokens(jax.random.fold_in(streams_of[13], 71), 0)
    segment = draw_segment(jax.random.fold_in(streams_of[13], 71), 0)
    attn_gain = jnp.clip(1.0 + 0.18 * jax.random.normal(streams_of[2], (D,), jnp.float32), 0.1, 1.9)
    w_query = draw_w_query(jax.random.fold_in(streams_of[13], 71), 0)
    w_key = draw_w_key(jax.random.fold_in(streams_of[13], 71), 0)
    w_value = bell_draw(streams_of[5], (D, KVH * HD), D ** -0.5, 0.15625)
    q_gain = draw_q_gain(jax.random.fold_in(streams_of[13], 71), 0)
    k_gain = draw_k_gain(jax.random.fold_in(streams_of[13], 71), 0)
    w_out = bell_draw(streams_of[8], (H * HD, D), (H * HD) ** -0.5, 0.15625)
    ffn_gain = jnp.clip(1.0 + 0.18 * jax.random.normal(streams_of[9], (D,), jnp.float32), 0.1, 1.9)
    w_gate = bell_draw(streams_of[10], (FF, D), D ** -0.5, 0.15625, ((0, 32),))
    w_up = bell_draw(streams_of[11], (FF, D), D ** -0.5, 0.15625, ((0, 32),))
    w_down = bell_draw(streams_of[12], (FF, D), FF ** -0.5, 0.09375, ((0, 32),))
    return dict(tokens=tokens, segment=segment, attn_gain=attn_gain, w_query=w_query, w_key=w_key, w_value=w_value, q_gain=q_gain, k_gain=k_gain, w_out=w_out, ffn_gain=ffn_gain, w_gate=w_gate, w_up=w_up, w_down=w_down)


EPSILON = 1e-05
ROPE_BASE = 1000000.0
NEG_FILL = -1e+30

def rms_scale(values, gain):
    mean_sq = lax.optimization_barrier(jnp.mean(values * values, axis=-1, keepdims=True))
    return values * lax.rsqrt(mean_sq + EPSILON) * gain

def seg_positions(seg_ids):
    indices = jnp.arange(seg_ids.shape[0], dtype=jnp.int32)
    is_first = jnp.concatenate([jnp.ones((1,), bool), seg_ids[1:] != seg_ids[:-1]])
    seg_begin = lax.cummax(jnp.where(is_first, indices, jnp.zeros_like(indices)), axis=0)
    return indices - seg_begin

def rotate(heads, positions):
    half_dim = heads.shape[-1] // 2
    inv_freq = ROPE_BASE ** (-(jnp.arange(half_dim, dtype=jnp.float32) * 2.0) / (2.0 * half_dim))
    angles = positions.astype(jnp.float32)[:, None] * inv_freq[None, :]
    cos_val = jnp.cos(angles)[:, None, :]
    sin_val = jnp.sin(angles)[:, None, :]
    left = heads[..., :half_dim]
    right = heads[..., half_dim:]
    return jnp.concatenate([left * cos_val - right * sin_val, right * cos_val + left * sin_val], axis=-1)

def attend_group(args):
    queries, key_heads, values, seg_ids = args
    count_rows = seg_ids.shape[0]
    groups = H // KVH
    indices = jnp.arange(count_rows, dtype=jnp.int32)
    allowed = (indices[None, :] <= indices[:, None]) & (seg_ids[None, :] == seg_ids[:, None])
    q_grid = queries.reshape(count_rows, KVH, groups, HD).transpose(1, 2, 0, 3)
    k_grid = key_heads.reshape(count_rows, KVH, HD).transpose(1, 0, 2)
    v_grid = values.reshape(count_rows, KVH, HD).transpose(1, 0, 2)

    def one_head(head_args):
        q_head, k_head, v_head = head_args
        scores = jnp.einsum('gqd,cd->gqc', q_head.astype(jnp.float32), k_head.astype(jnp.float32)) * 0.125
        scores = jnp.where(allowed[None], scores, NEG_FILL)
        peak = lax.optimization_barrier(jnp.max(scores, axis=-1, keepdims=True))
        weights = jnp.where(allowed[None], jnp.exp(scores - peak), 0.0)
        weight_sum = lax.optimization_barrier(jnp.sum(weights, axis=-1, keepdims=True))
        probs = lax.optimization_barrier(weights.astype(jnp.bfloat16)).astype(jnp.float32)
        return jnp.einsum('gqc,cd->gqd', probs, v_head.astype(jnp.float32)) / weight_sum
    out_heads = lax.map(one_head, (q_grid, k_grid, v_grid))
    return out_heads.transpose(2, 0, 1, 3).reshape(count_rows, H * HD).astype(jnp.bfloat16)

def reference(tokens, segment, attn_gain, w_query, w_key, w_value, q_gain, k_gain, w_out, ffn_gain, w_gate, w_up, w_down):
    count_rows = tokens.shape[0]
    positions = seg_positions(segment)
    resid = tokens.astype(jnp.float32)
    normed = rms_scale(resid, attn_gain).astype(jnp.bfloat16)
    q_raw = jnp.dot(normed, w_query, preferred_element_type=jnp.float32).reshape(count_rows, H, HD)
    k_raw = jnp.dot(normed, w_key, preferred_element_type=jnp.float32).reshape(count_rows, KVH, HD)
    queries = rotate(rms_scale(q_raw, q_gain), positions).astype(jnp.bfloat16)
    key_heads = rotate(rms_scale(k_raw, k_gain), positions).astype(jnp.bfloat16).reshape(count_rows, KVH * HD)
    values = jnp.dot(normed, w_value, preferred_element_type=jnp.float32).astype(jnp.bfloat16)
    kv_cache = jnp.concatenate([key_heads, values], axis=1)
    attended = lax.map(attend_group, (queries.reshape(N_REQ, GROUP_TOK, H, HD), key_heads.reshape(N_REQ, GROUP_TOK, KVH * HD), values.reshape(N_REQ, GROUP_TOK, KVH * HD), segment.reshape(N_REQ, GROUP_TOK)))
    attended = attended.reshape(count_rows, H * HD)
    after_attn = (resid + jnp.dot(attended, w_out, preferred_element_type=jnp.float32)).astype(jnp.bfloat16)
    after_f32 = lax.optimization_barrier(after_attn).astype(jnp.float32)
    mlp_in = rms_scale(after_f32, ffn_gain).astype(jnp.bfloat16)

    def mlp_group(rows_in):
        gate_act = jnp.dot(rows_in, w_gate.T, preferred_element_type=jnp.float32)
        up_act = jnp.dot(rows_in, w_up.T, preferred_element_type=jnp.float32)
        hidden = (jax.nn.silu(gate_act) * up_act).astype(jnp.bfloat16)
        return jnp.dot(hidden, w_down, preferred_element_type=jnp.float32)
    mlp_out = lax.map(mlp_group, mlp_in.reshape(N_REQ, GROUP_TOK, D)).reshape(count_rows, D)
    mixed = (after_f32 + mlp_out).astype(jnp.bfloat16)
    return (mixed, kv_cache)
```

```python
import functools

import jax
import jax.numpy as jnp
from jax import lax
from jax.experimental import pallas as pl
from jax.experimental.pallas import tpu as pltpu
from jax.sharding import PartitionSpec as P

H = 24
KVH = 8
HD = 64


EPSILON = 1e-05
ROPE_BASE = 1000000.0
NEG_FILL = -1e30
SCORE_SCALE = 0.125
MESH = pl.DeviceIdType.MESH
F32 = jnp.float32
BF16 = jnp.bfloat16


def rms_scale(values, gain):
    mean_sq = jnp.mean(values * values, axis=-1, keepdims=True)
    return values * lax.rsqrt(mean_sq + EPSILON) * gain


def rotate(heads, positions):
    half_dim = heads.shape[-1] // 2
    inv_freq = ROPE_BASE ** (-(jnp.arange(half_dim, dtype=jnp.float32) * 2.0) / (2.0 * half_dim))
    angles = positions.astype(jnp.float32)[:, None] * inv_freq[None, :]
    cos_val = jnp.cos(angles)[:, None, :]
    sin_val = jnp.sin(angles)[:, None, :]
    left = heads[..., :half_dim]
    right = heads[..., half_dim:]
    return jnp.concatenate(
        [left * cos_val - right * sin_val, right * cos_val + left * sin_val], axis=-1
    )


def attention_kernel(q_ref, k_ref, v_ref, seg_ref, own_ref, base_ref, o_ref, bias_ref):
    rows, keys = bias_ref.shape

    @pl.when(pl.program_id(0) == 0)
    def _():
        q_idx = base_ref[0] + lax.broadcasted_iota(jnp.int32, (rows, keys), 0)
        k_idx = lax.broadcasted_iota(jnp.int32, (rows, keys), 1)
        allowed = (k_idx <= q_idx) & (seg_ref[...] == own_ref[...])
        bias_ref[...] = jnp.where(allowed, 0.0, NEG_FILL)

    k = k_ref[...]
    v = v_ref[...]
    for j in range(2):
        for g in range(H // KVH):
            c = (j * (H // KVH) + g) * HD
            q = q_ref[:, c : c + HD]
            zero = jnp.zeros_like(q)
            q = jnp.concatenate([q, zero] if j == 0 else [zero, q], axis=1)
            s = lax.dot_general(q, k, (((1,), (1,)), ((), ())), preferred_element_type=F32)
            s = s * SCORE_SCALE + bias_ref[...]
            p = jnp.exp(s - jnp.max(s, axis=-1, keepdims=True))
            total = jnp.sum(p, axis=-1, keepdims=True)
            o = jnp.dot(p.astype(BF16), v, preferred_element_type=F32)
            o_ref[:, c : c + HD] = (o[:, j * HD : (j + 1) * HD] / total).astype(BF16)


def attention(queries, kv_all, group_seg, own_seg, row_base):
    rows = queries.shape[0]
    keys = kv_all.shape[0]
    pairs = KVH // 2
    wide = 2 * (H // KVH) * HD
    return pl.pallas_call(
        attention_kernel,
        grid=(pairs,),
        out_shape=jax.ShapeDtypeStruct((rows, H * HD), BF16),
        in_specs=[
            pl.BlockSpec((rows, wide), lambda i: (0, i)),
            pl.BlockSpec((keys, 2 * HD), lambda i: (0, i)),
            pl.BlockSpec((keys, 2 * HD), lambda i: (0, i + pairs)),
            pl.BlockSpec((1, keys), lambda i: (0, 0)),
            pl.BlockSpec((rows, 1), lambda i: (0, 0)),
            pl.BlockSpec(memory_space=pltpu.SMEM),
        ],
        out_specs=pl.BlockSpec((rows, wide), lambda i: (0, i)),
        scratch_shapes=[pltpu.VMEM((rows, keys), F32)],
        compiler_params=pltpu.CompilerParams(vmem_limit_bytes=40 * 1024 * 1024),
        cost_estimate=pl.CostEstimate(
            flops=16 * rows * keys * H * HD,
            bytes_accessed=4 * rows * H * HD + 4 * keys * KVH * HD,
            transcendentals=rows * keys * H,
        ),
    )(
        queries,
        kv_all,
        kv_all,
        group_seg[None, :],
        own_seg[:, None],
        jnp.reshape(row_base, (1,)).astype(jnp.int32),
    )


def kv_gather_kernel(nz, kv_ref, out_ref, own_sem, right_s, right_r, left_s, left_r, side_s, side_r):
    req = lax.axis_index("req")
    hid = lax.axis_index("hid")
    x = lax.rem(hid, 2)
    z = hid // 2
    side = (req, hid + 1 - 2 * x)
    up = (req, lax.rem(hid + 2, 2 * nz))
    down = (req, lax.rem(hid + 2 * nz - 2, 2 * nz))
    barrier = pltpu.get_barrier_semaphore()
    pl.semaphore_signal(barrier, inc=1, device_id=side, device_id_type=MESH)

    @pl.when(z + 1 < nz)
    def _():
        pl.semaphore_signal(barrier, inc=1, device_id=up, device_id_type=MESH)

    @pl.when(z > 0)
    def _():
        pl.semaphore_signal(barrier, inc=1, device_id=down, device_id_type=MESH)

    pl.semaphore_wait(barrier, 1 + jnp.where(z + 1 < nz, 1, 0) + jnp.where(z > 0, 1, 0))

    def right(zb, s):
        slot = 2 * zb + x
        return pltpu.make_async_remote_copy(
            src_ref=kv_ref if s == 0 else out_ref.at[slot],
            dst_ref=out_ref.at[slot],
            send_sem=right_s.at[s],
            recv_sem=right_r.at[s],
            device_id=up,
            device_id_type=MESH,
        )

    def left(zb, s):
        slot = 2 * zb + x
        return pltpu.make_async_remote_copy(
            src_ref=kv_ref if s == 0 else out_ref.at[slot],
            dst_ref=out_ref.at[slot],
            send_sem=left_s.at[s],
            recv_sem=left_r.at[s],
            device_id=down,
            device_id_type=MESH,
        )

    def across(zb, own=False):
        slot = 2 * zb + x
        return pltpu.make_async_remote_copy(
            src_ref=kv_ref if own else out_ref.at[slot],
            dst_ref=out_ref.at[slot],
            send_sem=side_s.at[zb],
            recv_sem=side_r.at[zb],
            device_id=side,
            device_id_type=MESH,
        )

    for s in range(nz - 1):
        if s > 0:
            @pl.when(z - s >= 0)
            def _(s=s):
                right(z - s, s - 1).wait_recv()

            @pl.when(z + s < nz)
            def _(s=s):
                left(z + s, s - 1).wait_recv()

        @pl.when((z - s >= 0) & (z + 1 < nz))
        def _(s=s):
            right(z - s, s).start()

        @pl.when((z + s < nz) & (z > 0))
        def _(s=s):
            left(z + s, s).start()

        if s == 0:
            across(z, True).start()
            pltpu.make_async_copy(kv_ref, out_ref.at[hid], own_sem).start()
        else:

            @pl.when(z - s >= 0)
            def _(s=s):
                across(z - s).start()

            @pl.when(z + s < nz)
            def _(s=s):
                across(z + s).start()

    last = nz - 1

    @pl.when(z - last >= 0)
    def _():
        right(z - last, last - 1).wait_recv()
        across(z - last).start()

    @pl.when(z + last < nz)
    def _():
        left(z + last, last - 1).wait_recv()
        across(z + last).start()

    for s in range(nz - 1):

        @pl.when((z - s >= 0) & (z + 1 < nz))
        def _(s=s):
            right(z - s, s).wait_send()

        @pl.when((z + s < nz) & (z > 0))
        def _(s=s):
            left(z + s, s).wait_send()

    for zb in range(nz):
        across(zb).wait_send()
        across(zb).wait_recv()
    pltpu.make_async_copy(kv_ref, out_ref.at[hid], own_sem).wait()


def kv_gather(kv, hids):
    rows, cols = kv.shape
    nz = hids // 2
    dma = pltpu.SemaphoreType.DMA
    out = pl.pallas_call(
        functools.partial(kv_gather_kernel, nz),
        out_shape=jax.ShapeDtypeStruct((hids, rows, cols), BF16),
        in_specs=[pl.BlockSpec(memory_space=pltpu.VMEM)],
        out_specs=pl.BlockSpec(memory_space=pltpu.VMEM),
        scratch_shapes=[
            dma,
            dma((nz - 1,)),
            dma((nz - 1,)),
            dma((nz - 1,)),
            dma((nz - 1,)),
            dma((nz,)),
            dma((nz,)),
        ],
        compiler_params=pltpu.CompilerParams(
            collective_id=1, has_side_effects=True, vmem_limit_bytes=24 * 1024 * 1024
        ),
        cost_estimate=pl.CostEstimate(flops=0, bytes_accessed=100_000_000, transcendentals=0),
    )(kv)
    return out.reshape(hids * rows, cols)


def ffn_kernel(
    x_ref, after_ref, wg_ref, wu_ref, wd_ref, o_ref,
    gat, acc, sendc, rc, sd, rd, sx, rx, sy, ry, send_sem, recv_sem, own_sem,
):
    req = lax.axis_index("req")
    hid = lax.axis_index("hid")
    rows = x_ref.shape[0]
    half = rows // 2
    core = (req + 1 - 2 * lax.rem(req, 2), hid)
    ydev = (lax.rem(req + 2, 4), hid)
    xdev = (req, hid + 1 - 2 * lax.rem(hid, 2))
    lo, hi = pl.ds(0, half), pl.ds(half, half)

    barrier = pltpu.get_barrier_semaphore()
    for dev in (core, xdev, ydev):
        pl.semaphore_signal(barrier, inc=1, device_id=dev, device_id_type=MESH)
    pl.semaphore_wait(barrier, 3)

    def copy(src, dst, sem, dev):
        return pltpu.make_async_remote_copy(
            src_ref=src,
            dst_ref=dst,
            send_sem=send_sem.at[sem],
            recv_sem=recv_sem.at[sem],
            device_id=dev,
            device_id_type=MESH,
        )

    to_core = copy(x_ref, gat.at[0, 1], 0, core)
    x_lo = copy(x_ref.at[lo], gat.at[1, 0, lo], 1, xdev)
    x_hi = copy(x_ref.at[hi], gat.at[1, 0, hi], 2, xdev)
    y_lo = copy(x_ref.at[lo], gat.at[2, 0, lo], 3, ydev)
    y_hi = copy(x_ref.at[hi], gat.at[2, 0, hi], 4, ydev)
    d_lo = copy(gat.at[1, 0, lo], gat.at[3, 0, lo], 5, ydev)
    d_hi = copy(gat.at[2, 0, hi], gat.at[3, 0, hi], 6, xdev)
    core_x = copy(gat.at[1, 0], gat.at[1, 1], 7, core)
    core_y = copy(gat.at[2, 0], gat.at[2, 1], 8, core)
    core_d = copy(gat.at[3, 0], gat.at[3, 1], 9, core)
    sd_lo = copy(sd.at[lo], rd.at[lo], 10, xdev)
    sd_hi = copy(sd.at[hi], rd.at[hi], 11, ydev)
    sx_lo = copy(sx.at[lo], rx.at[lo], 12, xdev)
    sx_hi = copy(sx.at[hi], rx.at[hi], 13, xdev)
    sy_lo = copy(sy.at[lo], ry.at[lo], 14, ydev)
    sy_hi = copy(sy.at[hi], ry.at[hi], 15, ydev)

    def part(pair):
        return copy(sendc.at[pair], rc.at[pair], 16 + pair, core)

    x_lo.start()
    y_hi.start()
    x_hi.start()
    y_lo.start()
    to_core.start()
    own = pltpu.make_async_copy(x_ref, gat.at[0, 0], own_sem)
    own.start()

    def step(pair, carry):
        @pl.when(pair == 0)
        def _():
            own.wait()
            to_core.wait_recv()

        @pl.when(pair == 1)
        def _():
            x_lo.wait_recv()
            d_lo.start()
            y_hi.wait_recv()
            d_hi.start()
            x_hi.wait_recv()
            core_x.start()
            y_lo.wait_recv()
            core_y.start()
            core_x.wait_recv()

        @pl.when(pair == 2)
        def _():
            core_y.wait_recv()

        @pl.when(pair == 3)
        def _():
            d_lo.wait_recv()
            d_hi.wait_recv()
            core_d.start()
            core_d.wait_recv()

        x = gat[pair].reshape(2 * rows, gat.shape[-1])
        units = wg_ref.shape[0]
        cut = units // 3
        nt = (((1,), (1,)), ((), ()))
        total = None
        for j in range(3):
            at = pl.ds(j * cut, cut)
            gate = lax.dot_general(x, wg_ref[at, :], nt, preferred_element_type=F32)
            up = lax.dot_general(x, wu_ref[at, :], nt, preferred_element_type=F32)
            hidden = (gate / (1.0 + jnp.exp(-gate)) * up).astype(BF16)
            term = jnp.dot(hidden, wd_ref[at, :], preferred_element_type=F32)
            total = term if total is None else total + term
        acc[pair] = total[:rows]
        sendc[pair] = total[rows:].astype(BF16)
        part(pair).start()

        @pl.when(pair == 2)
        def _():
            part(1).wait_recv()
            sx[lo, :] = (acc[1, lo, :] + rc[1, lo, :].astype(F32)).astype(BF16)
            sx_lo.start()

        @pl.when(pair == 3)
        def _():
            part(2).wait_recv()
            sy[hi, :] = (acc[2, hi, :] + rc[2, hi, :].astype(F32)).astype(BF16)
            sy_hi.start()

        return carry

    lax.fori_loop(0, 4, step, 0)

    part(3).wait_recv()
    sd[...] = (acc[3] + rc[3].astype(F32)).astype(BF16)
    sd_lo.start()
    sd_hi.start()
    part(0).wait_recv()
    acc[0] = acc[0] + rc[0].astype(F32) + after_ref[...].astype(F32)
    sd_lo.wait_recv()
    sy[lo, :] = (acc[2, lo, :] + rc[2, lo, :].astype(F32) + rd[lo, :].astype(F32)).astype(BF16)
    sy_lo.start()
    sd_hi.wait_recv()
    sx[hi, :] = (acc[1, hi, :] + rc[1, hi, :].astype(F32) + rd[hi, :].astype(F32)).astype(BF16)
    sx_hi.start()
    sx_lo.wait_recv()
    sy_hi.wait_recv()
    sy_lo.wait_recv()
    sx_hi.wait_recv()
    o_ref[...] = (acc[0] + rx[...].astype(F32) + ry[...].astype(F32)).astype(BF16)
    for sent in (
        to_core, x_lo, x_hi, y_lo, y_hi, d_lo, d_hi, core_x, core_y, core_d,
        sd_lo, sd_hi, sx_lo, sx_hi, sy_lo, sy_hi, part(0), part(1), part(2), part(3),
    ):
        sent.wait_send()


def ffn_cube(mlp_in, after_attn, w_gate, w_up, w_down):
    rows, width = mlp_in.shape
    vmem = pl.BlockSpec(memory_space=pltpu.VMEM)
    block = pltpu.VMEM((rows, width), BF16)
    return pl.pallas_call(
        ffn_kernel,
        out_shape=jax.ShapeDtypeStruct((rows, width), BF16),
        in_specs=[vmem] * 5,
        out_specs=vmem,
        scratch_shapes=[
            pltpu.VMEM((4, 2, rows, width), BF16),
            pltpu.VMEM((4, rows, width), F32),
            pltpu.VMEM((4, rows, width), BF16),
            pltpu.VMEM((4, rows, width), BF16),
            block,
            block,
            block,
            block,
            block,
            block,
            pltpu.SemaphoreType.DMA((20,)),
            pltpu.SemaphoreType.DMA((20,)),
            pltpu.SemaphoreType.DMA,
        ],
        compiler_params=pltpu.CompilerParams(
            collective_id=2, has_side_effects=True, vmem_limit_bytes=56 * 1024 * 1024
        ),
        cost_estimate=pl.CostEstimate(
            flops=6 * 8 * rows * width * w_gate.shape[0],
            bytes_accessed=100_000_000,
            transcendentals=0,
        ),
    )(mlp_in, after_attn, w_gate, w_up, w_down)


def unit_terms(pieces, gathered):
    gate_part, up_part, down_part = pieces
    contract = (((1,), (1,)), ((), ()))
    gate_act = lax.dot_general(gathered, gate_part, contract, preferred_element_type=jnp.float32)
    up_act = lax.dot_general(gathered, up_part, contract, preferred_element_type=jnp.float32)
    hidden = (jax.nn.silu(gate_act) * up_act).astype(jnp.bfloat16)
    return jnp.dot(hidden, down_part, preferred_element_type=jnp.float32)


def per_device(
    cube,
    hids,
    tokens,
    segment,
    attn_gain,
    w_query,
    w_key,
    w_value,
    q_gain,
    k_gain,
    w_out,
    ffn_gain,
    w_gate,
    w_up,
    w_down,
):
    shard_rows = tokens.shape[0]
    if cube:
        lines = [list(range(x, hids, 2)) for x in range(2)]
        weights = [
            lax.all_gather(w, "hid", axis=0, tiled=True, axis_index_groups=lines)
            for w in (w_gate, w_up, w_down)
        ]
    else:
        weights = [lax.all_gather(w, "req", axis=0, tiled=True) for w in (w_gate, w_up, w_down)]
    group_seg = lax.all_gather(segment, "hid", axis=0, tiled=True)
    row_base = lax.axis_index("hid") * shard_rows
    own_seg = segment
    first = jnp.sum((group_seg[None, :] < own_seg[:, None]).astype(jnp.int32), axis=1)
    positions = row_base + jnp.arange(shard_rows, dtype=jnp.int32) - first
    resid = tokens.astype(jnp.float32)
    normed = rms_scale(resid, attn_gain).astype(jnp.bfloat16)
    q_raw = jnp.dot(normed, w_query, preferred_element_type=jnp.float32).reshape(shard_rows, H, HD)
    k_raw = jnp.dot(normed, w_key, preferred_element_type=jnp.float32).reshape(shard_rows, KVH, HD)
    queries = rotate(rms_scale(q_raw, q_gain), positions).astype(jnp.bfloat16)
    key_heads = (
        rotate(rms_scale(k_raw, k_gain), positions)
        .astype(jnp.bfloat16)
        .reshape(shard_rows, KVH * HD)
    )
    values = jnp.dot(normed, w_value, preferred_element_type=jnp.float32).astype(jnp.bfloat16)
    kv_cache = jnp.concatenate([key_heads, values], axis=1)
    if cube:
        kv_all = kv_gather(kv_cache, hids)
    else:
        kv_all = lax.all_gather(kv_cache, "hid", axis=0, tiled=True)
    attended = attention(
        queries.reshape(shard_rows, H * HD), kv_all, group_seg, own_seg, row_base
    )
    after_attn = (resid + jnp.dot(attended, w_out, preferred_element_type=jnp.float32)).astype(
        jnp.bfloat16
    )
    after_f32 = lax.optimization_barrier(after_attn).astype(jnp.float32)
    mlp_in = rms_scale(after_f32, ffn_gain).astype(jnp.bfloat16)
    if cube:
        return (ffn_cube(mlp_in, after_attn, *weights), kv_cache)
    gathered = lax.all_gather(mlp_in, "hid", axis=0, tiled=True)
    unit_sum = unit_terms(weights, gathered)
    own_share = lax.psum_scatter(
        unit_sum.astype(jnp.bfloat16), "hid", scatter_dimension=0, tiled=True
    ).astype(jnp.float32)
    mixed = (after_f32 + own_share).astype(jnp.bfloat16)
    return (mixed, kv_cache)


def solution(mesh):
    placed = (
        P(("req", "hid"), None),
        P(("req", "hid")),
        P(),
        P(),
        P(),
        P(),
        P(),
        P(),
        P(),
        P(),
        P(("req", "hid"), None),
        P(("req", "hid"), None),
        P(("req", "hid"), None),
    )
    cube = mesh.shape["req"] == 4 and mesh.shape["hid"] == 8
    return jax.shard_map(
        functools.partial(per_device, cube, mesh.shape["hid"]),
        mesh=mesh,
        in_specs=placed,
        out_specs=(P(("req", "hid"), None), P(("req", "hid"), None)),
        check_vma=False,
    )
```

```python
import functools

import jax
import jax.numpy as jnp
from jax import lax
from jax.experimental import pallas as pl
from jax.experimental.pallas import tpu as pltpu
from jax.sharding import PartitionSpec as P

H = 24
KVH = 8
HD = 64


EPSILON = 1e-05
ROPE_BASE = 1000000.0
NEG_FILL = -1e30
SCORE_SCALE = 0.125
MESH = pl.DeviceIdType.MESH
F32 = jnp.float32
BF16 = jnp.bfloat16


def rms_scale(values, gain):
    mean_sq = jnp.mean(values * values, axis=-1, keepdims=True)
    return values * lax.rsqrt(mean_sq + EPSILON) * gain


def rotate(heads, positions):
    half_dim = heads.shape[-1] // 2
    inv_freq = ROPE_BASE ** (-(jnp.arange(half_dim, dtype=jnp.float32) * 2.0) / (2.0 * half_dim))
    angles = positions.astype(jnp.float32)[:, None] * inv_freq[None, :]
    cos_val = jnp.cos(angles)[:, None, :]
    sin_val = jnp.sin(angles)[:, None, :]
    left = heads[..., :half_dim]
    right = heads[..., half_dim:]
    return jnp.concatenate(
        [left * cos_val - right * sin_val, right * cos_val + left * sin_val], axis=-1
    )


def seg_gather_kernel(hids, seg_ref, out_ref, own_sem, send_sem, recv_sem):
    req = lax.axis_index("req")
    hid = lax.axis_index("hid")
    barrier = pltpu.get_barrier_semaphore()
    peers = [(req, lax.rem(hid + k, hids)) for k in range(1, hids)]
    for dev in peers:
        pl.semaphore_signal(barrier, inc=1, device_id=dev, device_id_type=MESH)
    own = pltpu.make_async_copy(seg_ref, out_ref.at[hid], own_sem)
    own.start()
    pl.semaphore_wait(barrier, hids - 1)
    copies = [
        pltpu.make_async_remote_copy(
            src_ref=seg_ref,
            dst_ref=out_ref.at[hid],
            send_sem=send_sem.at[k],
            recv_sem=recv_sem.at[k],
            device_id=dev,
            device_id_type=MESH,
        )
        for k, dev in enumerate(peers)
    ]
    for c in copies:
        c.start()
    for c in copies:
        c.wait()
    own.wait()


def seg_gather(segment, hids):
    rows = segment.shape[0]
    vmem = pl.BlockSpec(memory_space=pltpu.VMEM)
    out = pl.pallas_call(
        functools.partial(seg_gather_kernel, hids),
        out_shape=jax.ShapeDtypeStruct((hids, 1, rows), jnp.int32),
        in_specs=[vmem],
        out_specs=vmem,
        scratch_shapes=[
            pltpu.SemaphoreType.DMA,
            pltpu.SemaphoreType.DMA((hids - 1,)),
            pltpu.SemaphoreType.DMA((hids - 1,)),
        ],
        compiler_params=pltpu.CompilerParams(collective_id=1, has_side_effects=True),
    )(segment[None, :])
    return out.reshape(hids * rows)


def layer_kernel(
    q_ref, kv_ref, tok_ref, seg_ref, own_ref, gain_ref, wo_hbm, wg_hbm, wu_hbm, wd_hbm, o_ref,
    kvs, bias_ref, att, wo, wts, x_ref, after_ref,
    gat, acc, sendc, rc, sd, rd, sx, rx, sy, ry,
    send_sem, recv_sem, own_sem, w_send, w_recv, w_own,
    right_s, right_r, left_s, left_r, side_s, side_r,
):
    nz = 4
    req = lax.axis_index("req")
    hid = lax.axis_index("hid")
    x = lax.rem(hid, 2)
    z = hid // 2
    rows = q_ref.shape[0]
    keys = seg_ref.shape[1]
    half = rows // 2
    lo, hi = pl.ds(0, half), pl.ds(half, half)
    core = (req + 1 - 2 * lax.rem(req, 2), hid)
    ydev = (lax.rem(req + 2, 4), hid)
    xdev = (req, hid + 1 - 2 * x)
    zdev = (req, hid + 2 - 4 * lax.rem(z, 2))
    mirror = (req, 2 * (nz - 1 - z) + x)
    up = (req, lax.rem(hid + 2, 2 * nz))
    down = (req, lax.rem(hid + 2 * nz - 2, 2 * nz))

    barrier = pltpu.get_barrier_semaphore()
    for dev in (core, xdev, ydev, zdev, mirror):
        pl.semaphore_signal(barrier, inc=1, device_id=dev, device_id_type=MESH)
    load_wo = pltpu.make_async_copy(wo_hbm, wo, own_sem.at[0])
    load_wo.start()
    pl.semaphore_wait(barrier, 5)

    def remote(src, dst, s_sem, r_sem, dev):
        return pltpu.make_async_remote_copy(
            src_ref=src,
            dst_ref=dst,
            send_sem=s_sem,
            recv_sem=r_sem,
            device_id=dev,
            device_id_type=MESH,
        )

    def right(zb, s):
        slot = 2 * zb + x
        src = kv_ref if s == 0 else kvs.at[slot]
        return remote(src, kvs.at[slot], right_s.at[s], right_r.at[s], up)

    def left(zb, s):
        slot = 2 * zb + x
        src = kv_ref if s == 0 else kvs.at[slot]
        return remote(src, kvs.at[slot], left_s.at[s], left_r.at[s], down)

    def across(zb, own=False):
        slot = 2 * zb + x
        src = kv_ref if own else kvs.at[slot]
        return remote(src, kvs.at[slot], side_s.at[zb], side_r.at[zb], xdev)

    units = wg_hbm.shape[0]
    part_of = [pl.ds(k * units, units) for k in range(4)]
    w_local, w_y, w_z, w_zy = [], [], [], []
    for w, src in enumerate((wg_hbm, wu_hbm, wd_hbm)):
        w_local.append(pltpu.make_async_copy(src, wts.at[w, part_of[0]], w_own.at[w]))
        w_y.append(remote(src, wts.at[w, part_of[1]], w_send.at[3 * w], w_recv.at[3 * w], ydev))
        w_z.append(
            remote(src, wts.at[w, part_of[2]], w_send.at[3 * w + 1], w_recv.at[3 * w + 1], mirror)
        )
        w_zy.append(
            remote(
                wts.at[w, part_of[2]],
                wts.at[w, part_of[3]],
                w_send.at[3 * w + 2],
                w_recv.at[3 * w + 2],
                ydev,
            )
        )

    own_kv = pltpu.make_async_copy(kv_ref, kvs.at[hid], own_sem.at[1])
    for s in range(nz - 1):
        if s > 0:
            @pl.when(z - s >= 0)
            def _(s=s):
                right(z - s, s - 1).wait_recv()

            @pl.when(z + s < nz)
            def _(s=s):
                left(z + s, s - 1).wait_recv()

        @pl.when((z - s >= 0) & (z + 1 < nz))
        def _(s=s):
            right(z - s, s).start()

        @pl.when((z + s < nz) & (z > 0))
        def _(s=s):
            left(z + s, s).start()

        if s == 0:
            across(z, True).start()
            own_kv.start()
            for w in range(3):
                w_y[w].start()
        else:

            @pl.when(z - s >= 0)
            def _(s=s):
                across(z - s).start()

            @pl.when(z + s < nz)
            def _(s=s):
                across(z + s).start()

        w_z[s].start()
        w_local[s].start()
        if s == 0:
            q_idx = hid * rows + lax.broadcasted_iota(jnp.int32, (rows, keys), 0)
            k_idx = lax.broadcasted_iota(jnp.int32, (rows, keys), 1)
            allowed = (k_idx <= q_idx) & (seg_ref[...] == own_ref[...])
            bias_ref[...] = jnp.where(allowed, 0.0, NEG_FILL)

    last = nz - 1

    @pl.when(z - last >= 0)
    def _():
        right(z - last, last - 1).wait_recv()
        across(z - last).start()

    @pl.when(z + last < nz)
    def _():
        left(z + last, last - 1).wait_recv()
        across(z + last).start()

    w_z[0].wait_recv()
    w_zy[0].start()
    for zb in range(nz):
        across(zb).wait_recv()
    own_kv.wait()

    groups = H // KVH
    wide = 2 * groups * HD

    def heads(i, carry):
        k_at = pl.ds(pl.multiple_of(i * 2 * HD, 2 * HD), 2 * HD)
        v_at = pl.ds(pl.multiple_of(i * 2 * HD + KVH * HD, 2 * HD), 2 * HD)
        q_at = pl.ds(pl.multiple_of(i * wide, wide), wide)
        k = kvs[:, :, k_at].reshape(keys, 2 * HD)
        v = kvs[:, :, v_at].reshape(keys, 2 * HD)
        q_all = q_ref[:, q_at]
        outs = []
        for j in range(2):
            for g in range(groups):
                c = (j * groups + g) * HD
                q = q_all[:, c : c + HD]
                zero = jnp.zeros_like(q)
                q = jnp.concatenate([q, zero] if j == 0 else [zero, q], axis=1)
                s = lax.dot_general(q, k, (((1,), (1,)), ((), ())), preferred_element_type=F32)
                s = s * SCORE_SCALE + bias_ref[...]
                p = jnp.exp(s - jnp.max(s, axis=-1, keepdims=True))
                total = jnp.sum(p, axis=-1, keepdims=True)
                o = jnp.dot(p.astype(BF16), v, preferred_element_type=F32)
                outs.append((o[:, j * HD : (j + 1) * HD] / total).astype(BF16))
        att[:, q_at] = jnp.concatenate(outs, axis=1)

        @pl.when(i == 1)
        def _():
            w_z[1].wait_recv()
            w_zy[1].start()

        return carry

    lax.fori_loop(0, KVH // 2, heads, 0)

    load_wo.wait()
    after = tok_ref[...].astype(F32) + jnp.dot(att[...], wo[...], preferred_element_type=F32)
    after_ref[...] = after.astype(BF16)
    after = after_ref[...].astype(F32)
    mean_sq = jnp.mean(after * after, axis=-1, keepdims=True)
    x_ref[...] = (after * lax.rsqrt(mean_sq + EPSILON) * gain_ref[...]).astype(BF16)

    def copy(src, dst, sem, dev):
        return remote(src, dst, send_sem.at[sem], recv_sem.at[sem], dev)

    to_core = copy(x_ref, gat.at[0, 1], 0, core)
    x_lo = copy(x_ref.at[lo], gat.at[1, 0, lo], 1, xdev)
    x_hi = copy(x_ref.at[hi], gat.at[1, 0, hi], 2, xdev)
    y_lo = copy(x_ref.at[lo], gat.at[2, 0, lo], 3, zdev)
    y_hi = copy(x_ref.at[hi], gat.at[2, 0, hi], 4, zdev)
    d_lo = copy(gat.at[1, 0, lo], gat.at[3, 0, lo], 5, zdev)
    d_hi = copy(gat.at[2, 0, hi], gat.at[3, 0, hi], 6, xdev)
    core_x = copy(gat.at[1, 0], gat.at[1, 1], 7, core)
    core_y = copy(gat.at[2, 0], gat.at[2, 1], 8, core)
    core_d = copy(gat.at[3, 0], gat.at[3, 1], 9, core)
    sd_lo = copy(sd.at[lo], rd.at[lo], 10, xdev)
    sd_hi = copy(sd.at[hi], rd.at[hi], 11, zdev)
    sx_lo = copy(sx.at[lo], rx.at[lo], 12, xdev)
    sx_hi = copy(sx.at[hi], rx.at[hi], 13, xdev)
    sy_lo = copy(sy.at[lo], ry.at[lo], 14, zdev)
    sy_hi = copy(sy.at[hi], ry.at[hi], 15, zdev)

    def part(pair):
        return copy(sendc.at[pair], rc.at[pair], 16 + pair, core)

    x_lo.start()
    y_hi.start()
    x_hi.start()
    y_lo.start()
    to_core.start()
    own = pltpu.make_async_copy(x_ref, gat.at[0, 0], own_sem.at[2])
    own.start()
    w_z[2].wait_recv()
    w_zy[2].start()

    def step(pair, carry):
        @pl.when(pair == 0)
        def _():
            x_lo.wait_recv()
            d_lo.start()
            y_hi.wait_recv()
            d_hi.start()
            own.wait()
            to_core.wait_recv()
            for w in range(3):
                w_local[w].wait()
                w_y[w].wait_recv()
                w_zy[w].wait_recv()

        @pl.when(pair == 1)
        def _():
            x_hi.wait_recv()
            core_x.start()
            y_lo.wait_recv()
            core_y.start()
            core_x.wait_recv()

        @pl.when(pair == 2)
        def _():
            d_lo.wait_recv()
            d_hi.wait_recv()
            core_d.start()
            core_y.wait_recv()

        @pl.when(pair == 3)
        def _():
            core_d.wait_recv()

        xs = gat[pair].reshape(2 * rows, gat.shape[-1])
        cut = wts.shape[1] // 3
        nt = (((1,), (1,)), ((), ()))
        total = None
        for j in range(3):
            at = pl.ds(j * cut, cut)
            gate = lax.dot_general(xs, wts[0, at, :], nt, preferred_element_type=F32)
            up_act = lax.dot_general(xs, wts[1, at, :], nt, preferred_element_type=F32)
            hidden = (gate / (1.0 + jnp.exp(-gate)) * up_act).astype(BF16)
            term = jnp.dot(hidden, wts[2, at, :], preferred_element_type=F32)
            total = term if total is None else total + term
        acc[pair] = total[:rows]
        sendc[pair] = total[rows:].astype(BF16)
        part(pair).start()

        @pl.when(pair == 2)
        def _():
            part(1).wait_recv()
            sx[lo, :] = (acc[1, lo, :] + rc[1, lo, :].astype(F32)).astype(BF16)
            sx_lo.start()

        @pl.when(pair == 3)
        def _():
            part(2).wait_recv()
            sy[hi, :] = (acc[2, hi, :] + rc[2, hi, :].astype(F32)).astype(BF16)
            sy_hi.start()

        return carry

    lax.fori_loop(0, 4, step, 0)

    part(3).wait_recv()
    sd[...] = (acc[3] + rc[3].astype(F32)).astype(BF16)
    sd_lo.start()
    sd_hi.start()
    part(0).wait_recv()
    acc[0] = acc[0] + rc[0].astype(F32) + after_ref[...].astype(F32)
    sd_lo.wait_recv()
    sy[lo, :] = (acc[2, lo, :] + rc[2, lo, :].astype(F32) + rd[lo, :].astype(F32)).astype(BF16)
    sy_lo.start()
    sd_hi.wait_recv()
    sx[hi, :] = (acc[1, hi, :] + rc[1, hi, :].astype(F32) + rd[hi, :].astype(F32)).astype(BF16)
    sx_hi.start()
    sx_lo.wait_recv()
    sy_hi.wait_recv()
    sy_lo.wait_recv()
    sx_hi.wait_recv()
    o_ref[...] = (acc[0] + rx[...].astype(F32) + ry[...].astype(F32)).astype(BF16)

    for s in range(nz - 1):

        @pl.when((z - s >= 0) & (z + 1 < nz))
        def _(s=s):
            right(z - s, s).wait_send()

        @pl.when((z + s < nz) & (z > 0))
        def _(s=s):
            left(z + s, s).wait_send()

    for zb in range(nz):
        across(zb).wait_send()
    for sent in (
        to_core, x_lo, x_hi, y_lo, y_hi, d_lo, d_hi, core_x, core_y, core_d,
        sd_lo, sd_hi, sx_lo, sx_hi, sy_lo, sy_hi, part(0), part(1), part(2), part(3),
        *w_y, *w_z, *w_zy,
    ):
        sent.wait_send()


def layer(queries, kv, tokens, group_seg, own_seg, ffn_gain, w_out, w_gate, w_up, w_down):
    rows, width = tokens.shape
    keys = group_seg.shape[0]
    vmem = pl.BlockSpec(memory_space=pltpu.VMEM)
    hbm = pl.BlockSpec(memory_space=pl.ANY)
    dma = pltpu.SemaphoreType.DMA
    block = pltpu.VMEM((rows, width), BF16)
    blocks = pltpu.VMEM((4, rows, width), BF16)
    return pl.pallas_call(
        layer_kernel,
        out_shape=jax.ShapeDtypeStruct((rows, width), BF16),
        in_specs=[vmem] * 6 + [hbm] * 4,
        out_specs=vmem,
        scratch_shapes=[
            pltpu.VMEM((keys // rows, rows, kv.shape[1]), BF16),
            pltpu.VMEM((rows, keys), F32),
            pltpu.VMEM((rows, H * HD), BF16),
            pltpu.VMEM(w_out.shape, BF16),
            pltpu.VMEM((3, 4 * w_gate.shape[0], width), BF16),
            block,
            block,
            pltpu.VMEM((4, 2, rows, width), BF16),
            pltpu.VMEM((4, rows, width), F32),
            blocks,
            blocks,
            block,
            block,
            block,
            block,
            block,
            block,
            dma((20,)),
            dma((20,)),
            dma((3,)),
            dma((9,)),
            dma((9,)),
            dma((3,)),
            dma((3,)),
            dma((3,)),
            dma((3,)),
            dma((3,)),
            dma((4,)),
            dma((4,)),
        ],
        compiler_params=pltpu.CompilerParams(
            collective_id=2, has_side_effects=True, vmem_limit_bytes=60 * 1024 * 1024
        ),
        cost_estimate=pl.CostEstimate(
            flops=6 * 32 * rows * width * w_gate.shape[0],
            bytes_accessed=100_000_000,
            transcendentals=0,
        ),
    )(
        queries,
        kv,
        tokens,
        group_seg[None, :],
        own_seg[:, None],
        ffn_gain[None, :],
        w_out,
        w_gate,
        w_up,
        w_down,
    )


def attend(queries, kv_all, group_seg, own_seg, row_base):
    rows, keys = queries.shape[0], kv_all.shape[0]
    q_grid = queries.reshape(rows, KVH, H // KVH, HD).transpose(1, 2, 0, 3)
    kv_grid = kv_all.reshape(keys, 2, KVH, HD).transpose(1, 2, 0, 3)
    query_idx = row_base + jnp.arange(rows, dtype=jnp.int32)
    key_idx = jnp.arange(keys, dtype=jnp.int32)
    allowed = (key_idx[None, :] <= query_idx[:, None]) & (group_seg[None, :] == own_seg[:, None])

    def one_head(args):
        q, k, v = args
        scores = jnp.einsum("gqd,cd->gqc", q, k, preferred_element_type=F32) * SCORE_SCALE
        scores = jnp.where(allowed, scores, NEG_FILL)
        weights = jnp.exp(scores - jnp.max(scores, axis=-1, keepdims=True))
        product = jnp.einsum("gqc,cd->gqd", weights.astype(BF16), v, preferred_element_type=F32)
        return product / jnp.sum(weights, axis=-1, keepdims=True)

    heads = lax.map(one_head, (q_grid, kv_grid[0], kv_grid[1]))
    return heads.transpose(2, 0, 1, 3).reshape(rows, H * HD).astype(BF16)


def unit_terms(pieces, gathered):
    gate_part, up_part, down_part = pieces
    contract = (((1,), (1,)), ((), ()))
    gate_act = lax.dot_general(gathered, gate_part, contract, preferred_element_type=jnp.float32)
    up_act = lax.dot_general(gathered, up_part, contract, preferred_element_type=jnp.float32)
    hidden = (jax.nn.silu(gate_act) * up_act).astype(jnp.bfloat16)
    return jnp.dot(hidden, down_part, preferred_element_type=jnp.float32)


def per_device(
    cube,
    hids,
    tokens,
    segment,
    attn_gain,
    w_query,
    w_key,
    w_value,
    q_gain,
    k_gain,
    w_out,
    ffn_gain,
    w_gate,
    w_up,
    w_down,
):
    shard_rows = tokens.shape[0]
    if cube:
        group_seg = seg_gather(segment, hids)
    else:
        group_seg = lax.all_gather(segment, "hid", axis=0, tiled=True)
    row_base = lax.axis_index("hid") * shard_rows
    own_seg = segment
    first = jnp.sum((group_seg[None, :] < own_seg[:, None]).astype(jnp.int32), axis=1)
    positions = row_base + jnp.arange(shard_rows, dtype=jnp.int32) - first
    resid = tokens.astype(jnp.float32)
    normed = rms_scale(resid, attn_gain).astype(jnp.bfloat16)
    q_raw = jnp.dot(normed, w_query, preferred_element_type=jnp.float32).reshape(shard_rows, H, HD)
    k_raw = jnp.dot(normed, w_key, preferred_element_type=jnp.float32).reshape(shard_rows, KVH, HD)
    queries = rotate(rms_scale(q_raw, q_gain), positions).astype(jnp.bfloat16)
    key_heads = (
        rotate(rms_scale(k_raw, k_gain), positions)
        .astype(jnp.bfloat16)
        .reshape(shard_rows, KVH * HD)
    )
    values = jnp.dot(normed, w_value, preferred_element_type=jnp.float32).astype(jnp.bfloat16)
    kv_cache = jnp.concatenate([key_heads, values], axis=1)
    queries = queries.reshape(shard_rows, H * HD)
    if cube:
        mixed = layer(
            queries, kv_cache, tokens, group_seg, own_seg, ffn_gain, w_out, w_gate, w_up, w_down
        )
        return (mixed, kv_cache)
    kv_all = lax.all_gather(kv_cache, "hid", axis=0, tiled=True)
    attended = attend(queries, kv_all, group_seg, own_seg, row_base)
    after_attn = (resid + jnp.dot(attended, w_out, preferred_element_type=jnp.float32)).astype(
        jnp.bfloat16
    )
    after_f32 = lax.optimization_barrier(after_attn).astype(jnp.float32)
    mlp_in = rms_scale(after_f32, ffn_gain).astype(jnp.bfloat16)
    weights = [lax.all_gather(w, "req", axis=0, tiled=True) for w in (w_gate, w_up, w_down)]
    gathered = lax.all_gather(mlp_in, "hid", axis=0, tiled=True)
    unit_sum = unit_terms(weights, gathered)
    own_share = lax.psum_scatter(
        unit_sum.astype(jnp.bfloat16), "hid", scatter_dimension=0, tiled=True
    ).astype(jnp.float32)
    mixed = (after_f32 + own_share).astype(jnp.bfloat16)
    return (mixed, kv_cache)


def solution(mesh):
    placed = (
        P(("req", "hid"), None),
        P(("req", "hid")),
        P(),
        P(),
        P(),
        P(),
        P(),
        P(),
        P(),
        P(),
        P(("req", "hid"), None),
        P(("req", "hid"), None),
        P(("req", "hid"), None),
    )
    cube = mesh.shape["req"] == 4 and mesh.shape["hid"] == 8
    return jax.shard_map(
        functools.partial(per_device, cube, mesh.shape["hid"]),
        mesh=mesh,
        in_specs=placed,
        out_specs=(P(("req", "hid"), None), P(("req", "hid"), None)),
        check_vma=False,
    )
```

```python
import functools

import jax
import jax.numpy as jnp
from jax import lax
from jax.experimental import pallas as pl
from jax.experimental.pallas import tpu as pltpu
from jax.sharding import PartitionSpec as P

H = 24
KVH = 8
HD = 64


EPSILON = 1e-05
ROPE_BASE = 1000000.0
NEG_FILL = -1e30
SCORE_SCALE = 0.125
MESH = pl.DeviceIdType.MESH
F32 = jnp.float32
BF16 = jnp.bfloat16


def rms_scale(values, gain):
    mean_sq = jnp.mean(values * values, axis=-1, keepdims=True)
    return values * lax.rsqrt(mean_sq + EPSILON) * gain


def rotate(heads, positions):
    half_dim = heads.shape[-1] // 2
    inv_freq = ROPE_BASE ** (-(jnp.arange(half_dim, dtype=jnp.float32) * 2.0) / (2.0 * half_dim))
    angles = positions.astype(jnp.float32)[:, None] * inv_freq[None, :]
    cos_val = jnp.cos(angles)[:, None, :]
    sin_val = jnp.sin(angles)[:, None, :]
    left = heads[..., :half_dim]
    right = heads[..., half_dim:]
    return jnp.concatenate(
        [left * cos_val - right * sin_val, right * cos_val + left * sin_val], axis=-1
    )


def seg_gather_kernel(hids, seg_ref, out_ref, own_sem, send_sem, recv_sem):
    req = lax.axis_index("req")
    hid = lax.axis_index("hid")
    barrier = pltpu.get_barrier_semaphore()
    peers = [(req, lax.rem(hid + k, hids)) for k in range(1, hids)]
    for dev in peers:
        pl.semaphore_signal(barrier, inc=1, device_id=dev, device_id_type=MESH)
    own = pltpu.make_async_copy(seg_ref, out_ref.at[hid], own_sem)
    own.start()
    pl.semaphore_wait(barrier, hids - 1)
    copies = [
        pltpu.make_async_remote_copy(
            src_ref=seg_ref,
            dst_ref=out_ref.at[hid],
            send_sem=send_sem.at[k],
            recv_sem=recv_sem.at[k],
            device_id=dev,
            device_id_type=MESH,
        )
        for k, dev in enumerate(peers)
    ]
    for c in copies:
        c.start()
    for c in copies:
        c.wait()
    own.wait()


def seg_gather(segment, hids):
    rows = segment.shape[0]
    vmem = pl.BlockSpec(memory_space=pltpu.VMEM)
    out = pl.pallas_call(
        functools.partial(seg_gather_kernel, hids),
        out_shape=jax.ShapeDtypeStruct((hids, 1, rows), jnp.int32),
        in_specs=[vmem],
        out_specs=vmem,
        scratch_shapes=[
            pltpu.SemaphoreType.DMA,
            pltpu.SemaphoreType.DMA((hids - 1,)),
            pltpu.SemaphoreType.DMA((hids - 1,)),
        ],
        compiler_params=pltpu.CompilerParams(collective_id=1, has_side_effects=True),
    )(segment[None, :])
    return out.reshape(hids * rows)


def layer_kernel(
    q_ref, kv_ref, tok_ref, seg_ref, own_ref, gain_ref, wo_hbm, wg_hbm, wu_hbm, wd_hbm, o_ref,
    kvs, bias_ref, att, wo, wts, x_ref, after_ref,
    gat, acc, sendc, rc, sd, rd, sx, rx, sy, ry,
    send_sem, recv_sem, own_sem, w_send, w_recv, w_own,
    right_s, right_r, left_s, left_r, side_s, side_r,
):
    nz = 4
    req = lax.axis_index("req")
    hid = lax.axis_index("hid")
    x = lax.rem(hid, 2)
    z = hid // 2
    rows = q_ref.shape[0]
    keys = seg_ref.shape[1]
    half = rows // 2
    lo, hi = pl.ds(0, half), pl.ds(half, half)
    core = (req + 1 - 2 * lax.rem(req, 2), hid)
    ydev = (lax.rem(req + 2, 4), hid)
    xdev = (req, hid + 1 - 2 * x)
    zdev = (req, hid + 2 - 4 * lax.rem(z, 2))
    mirror = (req, 2 * (nz - 1 - z) + x)
    up = (req, lax.rem(hid + 2, 2 * nz))
    down = (req, lax.rem(hid + 2 * nz - 2, 2 * nz))

    barrier = pltpu.get_barrier_semaphore()
    for dev in (core, xdev, ydev, zdev, mirror):
        pl.semaphore_signal(barrier, inc=1, device_id=dev, device_id_type=MESH)
    load_wo = pltpu.make_async_copy(wo_hbm, wo, own_sem.at[0])
    load_wo.start()
    pl.semaphore_wait(barrier, 5)

    def remote(src, dst, s_sem, r_sem, dev):
        return pltpu.make_async_remote_copy(
            src_ref=src,
            dst_ref=dst,
            send_sem=s_sem,
            recv_sem=r_sem,
            device_id=dev,
            device_id_type=MESH,
        )

    def right(zb, s):
        slot = 2 * zb + x
        src = kv_ref if s == 0 else kvs.at[slot]
        return remote(src, kvs.at[slot], right_s.at[s], right_r.at[s], up)

    def left(zb, s):
        slot = 2 * zb + x
        src = kv_ref if s == 0 else kvs.at[slot]
        return remote(src, kvs.at[slot], left_s.at[s], left_r.at[s], down)

    def across(zb, own=False):
        slot = 2 * zb + x
        src = kv_ref if own else kvs.at[slot]
        return remote(src, kvs.at[slot], side_s.at[zb], side_r.at[zb], xdev)

    units = wg_hbm.shape[0]
    part_of = [pl.ds(k * units, units) for k in range(4)]
    w_local, w_y, w_z, w_zy = [], [], [], []
    for w, src in enumerate((wg_hbm, wu_hbm, wd_hbm)):
        w_local.append(pltpu.make_async_copy(src, wts.at[w, part_of[0]], w_own.at[w]))
        w_y.append(remote(src, wts.at[w, part_of[1]], w_send.at[3 * w], w_recv.at[3 * w], ydev))
        w_z.append(
            remote(src, wts.at[w, part_of[2]], w_send.at[3 * w + 1], w_recv.at[3 * w + 1], mirror)
        )
        w_zy.append(
            remote(
                wts.at[w, part_of[2]],
                wts.at[w, part_of[3]],
                w_send.at[3 * w + 2],
                w_recv.at[3 * w + 2],
                ydev,
            )
        )

    own_kv = pltpu.make_async_copy(kv_ref, kvs.at[hid], own_sem.at[1])
    for s in range(nz - 1):
        if s > 0:
            @pl.when(z - s >= 0)
            def _(s=s):
                right(z - s, s - 1).wait_recv()

            @pl.when(z + s < nz)
            def _(s=s):
                left(z + s, s - 1).wait_recv()

        @pl.when((z - s >= 0) & (z + 1 < nz))
        def _(s=s):
            right(z - s, s).start()

        @pl.when((z + s < nz) & (z > 0))
        def _(s=s):
            left(z + s, s).start()

        if s == 0:
            across(z, True).start()
            own_kv.start()
            for w in range(3):
                w_y[w].start()
        else:

            @pl.when(z - s >= 0)
            def _(s=s):
                across(z - s).start()

            @pl.when(z + s < nz)
            def _(s=s):
                across(z + s).start()

        w_local[s].start()
        if s == 0:
            q_idx = hid * rows + lax.broadcasted_iota(jnp.int32, (rows, keys), 0)
            k_idx = lax.broadcasted_iota(jnp.int32, (rows, keys), 1)
            allowed = (k_idx <= q_idx) & (seg_ref[...] == own_ref[...])
            bias_ref[...] = jnp.where(allowed, 0.0, NEG_FILL)

    last = nz - 1

    @pl.when(z - last >= 0)
    def _():
        right(z - last, last - 1).wait_recv()
        across(z - last).start()

    @pl.when(z + last < nz)
    def _():
        left(z + last, last - 1).wait_recv()
        across(z + last).start()

    for w in range(3):
        w_z[w].start()
    for zb in range(nz):
        across(zb).wait_recv()
    own_kv.wait()

    groups = H // KVH
    wide = 2 * groups * HD

    def heads(i, carry):
        k_at = pl.ds(pl.multiple_of(i * 2 * HD, 2 * HD), 2 * HD)
        v_at = pl.ds(pl.multiple_of(i * 2 * HD + KVH * HD, 2 * HD), 2 * HD)
        q_at = pl.ds(pl.multiple_of(i * wide, wide), wide)
        k = kvs[:, :, k_at].reshape(keys, 2 * HD)
        v = kvs[:, :, v_at].reshape(keys, 2 * HD)
        q_all = q_ref[:, q_at]
        outs = []
        for j in range(2):
            for g in range(groups):
                c = (j * groups + g) * HD
                q = q_all[:, c : c + HD]
                zero = jnp.zeros_like(q)
                q = jnp.concatenate([q, zero] if j == 0 else [zero, q], axis=1)
                s = lax.dot_general(q, k, (((1,), (1,)), ((), ())), preferred_element_type=F32)
                s = s * SCORE_SCALE + bias_ref[...]
                p = jnp.exp(s - jnp.max(s, axis=-1, keepdims=True))
                total = jnp.sum(p, axis=-1, keepdims=True)
                o = jnp.dot(p.astype(BF16), v, preferred_element_type=F32)
                outs.append((o[:, j * HD : (j + 1) * HD] / total).astype(BF16))
        att[:, q_at] = jnp.concatenate(outs, axis=1)

        @pl.when(i == 2)
        def _():
            w_z[0].wait_recv()
            w_zy[0].start()

        @pl.when(i == 3)
        def _():
            w_z[1].wait_recv()
            w_zy[1].start()

        return carry

    lax.fori_loop(0, KVH // 2, heads, 0)

    load_wo.wait()
    after = tok_ref[...].astype(F32) + jnp.dot(att[...], wo[...], preferred_element_type=F32)
    after_ref[...] = after.astype(BF16)
    after = after_ref[...].astype(F32)
    mean_sq = jnp.mean(after * after, axis=-1, keepdims=True)
    x_ref[...] = (after * lax.rsqrt(mean_sq + EPSILON) * gain_ref[...]).astype(BF16)

    def copy(src, dst, sem, dev):
        return remote(src, dst, send_sem.at[sem], recv_sem.at[sem], dev)

    to_core = copy(x_ref, gat.at[0, 1], 0, core)
    x_lo = copy(x_ref.at[lo], gat.at[1, 0, lo], 1, xdev)
    x_hi = copy(x_ref.at[hi], gat.at[1, 0, hi], 2, xdev)
    y_lo = copy(x_ref.at[lo], gat.at[2, 0, lo], 3, zdev)
    y_hi = copy(x_ref.at[hi], gat.at[2, 0, hi], 4, zdev)
    d_lo = copy(gat.at[1, 0, lo], gat.at[3, 0, lo], 5, zdev)
    d_hi = copy(gat.at[2, 0, hi], gat.at[3, 0, hi], 6, xdev)
    core_x = copy(gat.at[1, 0], gat.at[1, 1], 7, core)
    core_y = copy(gat.at[2, 0], gat.at[2, 1], 8, core)
    core_d = copy(gat.at[3, 0], gat.at[3, 1], 9, core)
    sd_lo = copy(sd.at[lo], rd.at[lo], 10, xdev)
    sd_hi = copy(sd.at[hi], rd.at[hi], 11, zdev)
    sx_lo = copy(sx.at[lo], rx.at[lo], 12, xdev)
    sx_hi = copy(sx.at[hi], rx.at[hi], 13, xdev)
    sy_lo = copy(sy.at[lo], ry.at[lo], 14, zdev)
    sy_hi = copy(sy.at[hi], ry.at[hi], 15, zdev)

    def part(pair):
        return copy(sendc.at[pair], rc.at[pair], 16 + pair, core)

    x_lo.start()
    y_hi.start()
    x_hi.start()
    y_lo.start()
    to_core.start()
    own = pltpu.make_async_copy(x_ref, gat.at[0, 0], own_sem.at[2])
    own.start()
    w_z[2].wait_recv()
    w_zy[2].start()

    def step(pair, carry):
        @pl.when(pair == 0)
        def _():
            x_lo.wait_recv()
            d_lo.start()
            y_hi.wait_recv()
            d_hi.start()
            own.wait()
            to_core.wait_recv()
            for w in range(3):
                w_local[w].wait()
                w_y[w].wait_recv()
                w_zy[w].wait_recv()

        @pl.when(pair == 1)
        def _():
            x_hi.wait_recv()
            core_x.start()
            y_lo.wait_recv()
            core_y.start()
            core_x.wait_recv()

        @pl.when(pair == 2)
        def _():
            d_lo.wait_recv()
            d_hi.wait_recv()
            core_d.start()
            core_y.wait_recv()

        @pl.when(pair == 3)
        def _():
            core_d.wait_recv()

        xs = gat[pair].reshape(2 * rows, gat.shape[-1])
        cut = wts.shape[1] // 3
        nt = (((1,), (1,)), ((), ()))
        total = None
        for j in range(3):
            at = pl.ds(j * cut, cut)
            gate = lax.dot_general(xs, wts[0, at, :], nt, preferred_element_type=F32)
            up_act = lax.dot_general(xs, wts[1, at, :], nt, preferred_element_type=F32)
            hidden = (gate / (1.0 + jnp.exp(-gate)) * up_act).astype(BF16)
            term = jnp.dot(hidden, wts[2, at, :], preferred_element_type=F32)
            total = term if total is None else total + term
        acc[pair] = total[:rows]
        sendc[pair] = total[rows:].astype(BF16)
        part(pair).start()

        @pl.when(pair == 2)
        def _():
            part(1).wait_recv()
            sx[lo, :] = (acc[1, lo, :] + rc[1, lo, :].astype(F32)).astype(BF16)
            sx_lo.start()

        @pl.when(pair == 3)
        def _():
            part(2).wait_recv()
            sy[hi, :] = (acc[2, hi, :] + rc[2, hi, :].astype(F32)).astype(BF16)
            sy_hi.start()

        return carry

    lax.fori_loop(0, 4, step, 0)

    part(3).wait_recv()
    sd[...] = (acc[3] + rc[3].astype(F32)).astype(BF16)
    sd_lo.start()
    sd_hi.start()
    part(0).wait_recv()
    acc[0] = acc[0] + rc[0].astype(F32) + after_ref[...].astype(F32)
    sd_lo.wait_recv()
    sy[lo, :] = (acc[2, lo, :] + rc[2, lo, :].astype(F32) + rd[lo, :].astype(F32)).astype(BF16)
    sy_lo.start()
    sd_hi.wait_recv()
    sx[hi, :] = (acc[1, hi, :] + rc[1, hi, :].astype(F32) + rd[hi, :].astype(F32)).astype(BF16)
    sx_hi.start()
    sx_lo.wait_recv()
    sy_hi.wait_recv()
    sy_lo.wait_recv()
    sx_hi.wait_recv()
    o_ref[...] = (acc[0] + rx[...].astype(F32) + ry[...].astype(F32)).astype(BF16)

    for s in range(nz - 1):

        @pl.when((z - s >= 0) & (z + 1 < nz))
        def _(s=s):
            right(z - s, s).wait_send()

        @pl.when((z + s < nz) & (z > 0))
        def _(s=s):
            left(z + s, s).wait_send()

    for zb in range(nz):
        across(zb).wait_send()
    for sent in (
        to_core, x_lo, x_hi, y_lo, y_hi, d_lo, d_hi, core_x, core_y, core_d,
        sd_lo, sd_hi, sx_lo, sx_hi, sy_lo, sy_hi, part(0), part(1), part(2), part(3),
        *w_y, *w_z, *w_zy,
    ):
        sent.wait_send()


def layer(queries, kv, tokens, group_seg, own_seg, ffn_gain, w_out, w_gate, w_up, w_down):
    rows, width = tokens.shape
    keys = group_seg.shape[0]
    vmem = pl.BlockSpec(memory_space=pltpu.VMEM)
    hbm = pl.BlockSpec(memory_space=pl.ANY)
    dma = pltpu.SemaphoreType.DMA
    block = pltpu.VMEM((rows, width), BF16)
    blocks = pltpu.VMEM((4, rows, width), BF16)
    return pl.pallas_call(
        layer_kernel,
        out_shape=jax.ShapeDtypeStruct((rows, width), BF16),
        in_specs=[vmem] * 6 + [hbm] * 4,
        out_specs=vmem,
        scratch_shapes=[
            pltpu.VMEM((keys // rows, rows, kv.shape[1]), BF16),
            pltpu.VMEM((rows, keys), F32),
            pltpu.VMEM((rows, H * HD), BF16),
            pltpu.VMEM(w_out.shape, BF16),
            pltpu.VMEM((3, 4 * w_gate.shape[0], width), BF16),
            block,
            block,
            pltpu.VMEM((4, 2, rows, width), BF16),
            pltpu.VMEM((4, rows, width), F32),
            blocks,
            blocks,
            block,
            block,
            block,
            block,
            block,
            block,
            dma((20,)),
            dma((20,)),
            dma((3,)),
            dma((9,)),
            dma((9,)),
            dma((3,)),
            dma((3,)),
            dma((3,)),
            dma((3,)),
            dma((3,)),
            dma((4,)),
            dma((4,)),
        ],
        compiler_params=pltpu.CompilerParams(
            collective_id=2, has_side_effects=True, vmem_limit_bytes=60 * 1024 * 1024
        ),
        cost_estimate=pl.CostEstimate(
            flops=6 * 32 * rows * width * w_gate.shape[0],
            bytes_accessed=100_000_000,
            transcendentals=0,
        ),
    )(
        queries,
        kv,
        tokens,
        group_seg[None, :],
        own_seg[:, None],
        ffn_gain[None, :],
        w_out,
        w_gate,
        w_up,
        w_down,
    )


def attend(queries, kv_all, group_seg, own_seg, row_base):
    rows, keys = queries.shape[0], kv_all.shape[0]
    q_grid = queries.reshape(rows, KVH, H // KVH, HD).transpose(1, 2, 0, 3)
    kv_grid = kv_all.reshape(keys, 2, KVH, HD).transpose(1, 2, 0, 3)
    query_idx = row_base + jnp.arange(rows, dtype=jnp.int32)
    key_idx = jnp.arange(keys, dtype=jnp.int32)
    allowed = (key_idx[None, :] <= query_idx[:, None]) & (group_seg[None, :] == own_seg[:, None])

    def one_head(args):
        q, k, v = args
        scores = jnp.einsum("gqd,cd->gqc", q, k, preferred_element_type=F32) * SCORE_SCALE
        scores = jnp.where(allowed, scores, NEG_FILL)
        weights = jnp.exp(scores - jnp.max(scores, axis=-1, keepdims=True))
        product = jnp.einsum("gqc,cd->gqd", weights.astype(BF16), v, preferred_element_type=F32)
        return product / jnp.sum(weights, axis=-1, keepdims=True)

    heads = lax.map(one_head, (q_grid, kv_grid[0], kv_grid[1]))
    return heads.transpose(2, 0, 1, 3).reshape(rows, H * HD).astype(BF16)


def unit_terms(pieces, gathered):
    gate_part, up_part, down_part = pieces
    contract = (((1,), (1,)), ((), ()))
    gate_act = lax.dot_general(gathered, gate_part, contract, preferred_element_type=jnp.float32)
    up_act = lax.dot_general(gathered, up_part, contract, preferred_element_type=jnp.float32)
    hidden = (jax.nn.silu(gate_act) * up_act).astype(jnp.bfloat16)
    return jnp.dot(hidden, down_part, preferred_element_type=jnp.float32)


def per_device(
    cube,
    hids,
    tokens,
    segment,
    attn_gain,
    w_query,
    w_key,
    w_value,
    q_gain,
    k_gain,
    w_out,
    ffn_gain,
    w_gate,
    w_up,
    w_down,
):
    shard_rows = tokens.shape[0]
    if cube:
        group_seg = seg_gather(segment, hids)
    else:
        group_seg = lax.all_gather(segment, "hid", axis=0, tiled=True)
    row_base = lax.axis_index("hid") * shard_rows
    own_seg = segment
    first = jnp.sum((group_seg[None, :] < own_seg[:, None]).astype(jnp.int32), axis=1)
    positions = row_base + jnp.arange(shard_rows, dtype=jnp.int32) - first
    resid = tokens.astype(jnp.float32)
    normed = rms_scale(resid, attn_gain).astype(jnp.bfloat16)
    q_raw = jnp.dot(normed, w_query, preferred_element_type=jnp.float32).reshape(shard_rows, H, HD)
    k_raw = jnp.dot(normed, w_key, preferred_element_type=jnp.float32).reshape(shard_rows, KVH, HD)
    queries = rotate(rms_scale(q_raw, q_gain), positions).astype(jnp.bfloat16)
    key_heads = (
        rotate(rms_scale(k_raw, k_gain), positions)
        .astype(jnp.bfloat16)
        .reshape(shard_rows, KVH * HD)
    )
    values = jnp.dot(normed, w_value, preferred_element_type=jnp.float32).astype(jnp.bfloat16)
    kv_cache = jnp.concatenate([key_heads, values], axis=1)
    queries = queries.reshape(shard_rows, H * HD)
    if cube:
        mixed = layer(
            queries, kv_cache, tokens, group_seg, own_seg, ffn_gain, w_out, w_gate, w_up, w_down
        )
        return (mixed, kv_cache)
    kv_all = lax.all_gather(kv_cache, "hid", axis=0, tiled=True)
    attended = attend(queries, kv_all, group_seg, own_seg, row_base)
    after_attn = (resid + jnp.dot(attended, w_out, preferred_element_type=jnp.float32)).astype(
        jnp.bfloat16
    )
    after_f32 = lax.optimization_barrier(after_attn).astype(jnp.float32)
    mlp_in = rms_scale(after_f32, ffn_gain).astype(jnp.bfloat16)
    weights = [lax.all_gather(w, "req", axis=0, tiled=True) for w in (w_gate, w_up, w_down)]
    gathered = lax.all_gather(mlp_in, "hid", axis=0, tiled=True)
    unit_sum = unit_terms(weights, gathered)
    own_share = lax.psum_scatter(
        unit_sum.astype(jnp.bfloat16), "hid", scatter_dimension=0, tiled=True
    ).astype(jnp.float32)
    mixed = (after_f32 + own_share).astype(jnp.bfloat16)
    return (mixed, kv_cache)


def solution(mesh):
    placed = (
        P(("req", "hid"), None),
        P(("req", "hid")),
        P(),
        P(),
        P(),
        P(),
        P(),
        P(),
        P(),
        P(),
        P(("req", "hid"), None),
        P(("req", "hid"), None),
        P(("req", "hid"), None),
    )
    cube = mesh.shape["req"] == 4 and mesh.shape["hid"] == 8
    return jax.shard_map(
        functools.partial(per_device, cube, mesh.shape["hid"]),
        mesh=mesh,
        in_specs=placed,
        out_specs=(P(("req", "hid"), None), P(("req", "hid"), None)),
        check_vma=False,
    )
```
